32 devices in a mesh: blk: 16 (over z, y, core), band: 2 (over x).
Axes of the slice: x: 2, y: 2, z: 4, core: 2. Of those that a mesh axis runs over, the one named last changes fastest.
Arguments:
- spectra: bfloat16 [32, 3, 2, 320], P('blk', None, None, 'band'), may hold values from -6 to 6
- quality: int32 [32, 3], P('blk'), may hold values 0 or 1
Outputs:
- correlations: bfloat16 [16, 32, 2, 9, 128], P(None, 'blk', 'band')
The draws below stay inside these ranges and needn't reach their ends.
All inputs are finite; a program needn't handle non-finite values. No bound on the sum of `quality` on one device may be relied on, other than what follows from the above.
Results may differ from the reference program's by a relative error of at most 0.0012.
Values may be sent and summed in bfloat16 or wider, within the bound.
No kernel may reach another device: no remote copies, remote signals or barrier semaphores. Data moves between devices by JAX's collectives and lax.ppermute only.
A program may use at most 64 MiB of HBM per device.

```python
import math
import jax
import jax.numpy as jnp
from jax import lax

F = 320
FIRST = 15
NFFT = 1500
MAXLAG = 64
LAGS = 128
TILE = 2
STATIONS = 32
N_BLK = 16


def with_ends(entries, stream_key, smallest, high):
    index_at = [jax.random.randint(jax.random.fold_in(stream_key, axis), (), 0, length) for axis, length in enumerate(entries.shape)]
    longest = entries.shape.index(max(entries.shape))
    next_to = index_at[:longest] + [(index_at[longest] + 1) % entries.shape[longest]] + index_at[longest + 1:]
    return entries.at[tuple(index_at)].set(smallest).at[tuple(next_to)].set(high)


def steps_of(stream_key, dims, split, least, largest):
    def one(dim, shards_of):
        draws = jax.random.uniform(jax.random.fold_in(jax.random.fold_in(stream_key, 6), dim), (shards_of,), jnp.float32, least / len(split), largest / len(split))
        return jnp.repeat(jnp.exp(draws), dims[dim] // shards_of).reshape((-1,) + (1,) * (len(dims) - dim - 1))

    gain = one(*split[0])
    for cut in split[1:]:
        gain = gain * one(*cut)
    return gain


def bell_draw(own_key, shape, spread, limit, split=(), kind=jnp.bfloat16):
    entries = jax.random.normal(own_key, shape, jnp.float32) * spread
    if len(split) > 0:
        entries = steps_of(own_key, shape, split, -0.22, 0.18) * entries
    return jnp.clip(entries, min=-limit, max=limit).astype(kind)


def setup_inputs(seed: int = 0) -> dict:
    key_list = jax.random.split(jax.random.key(seed), 3)
    return {
        "spectra": bell_draw(key_list[0], (STATIONS, 3, 2, F), 1.0, 6.0, ((0, 16), (3, 2))),
        "quality": with_ends((jax.random.randint(key_list[1], (STATIONS, 3), 0, 8) < 7).astype(jnp.int32), jax.random.fold_in(key_list[1], 1), 0, 1),
    }


def lag_transform():
    bins = jnp.arange(F, dtype=jnp.int32) + FIRST
    lag_steps = 2 * jnp.arange(LAGS, dtype=jnp.int32) - 2 * MAXLAG + 1
    phase_index = bins[:, None] * lag_steps[None, :] % (2 * NFFT)
    phases = math.pi / NFFT * phase_index.astype(jnp.float32)
    factor = 1.0 / math.sqrt(F)
    return jnp.stack([jnp.cos(phases) * factor, -jnp.sin(phases) * factor], axis=0)

def cross_spectra(left, right):
    left_count = left.shape[0]
    right_count = right.shape[0]
    bin_count = left.shape[3]
    left_real = left[:, :, 0, :][:, None, :, None, :]
    left_imag = left[:, :, 1, :][:, None, :, None, :]
    right_real = right[:, :, 0, :][None, :, None, :, :]
    right_imag = right[:, :, 1, :][None, :, None, :, :]
    real_part = left_real * right_real + left_imag * right_imag
    imag_part = left_imag * right_real - left_real * right_imag
    products = jnp.stack([real_part, imag_part], axis=4)
    return products.reshape(left_count * right_count * 9, 2 * bin_count)

def reference(spectra, quality):
    masked = (spectra * quality.astype(jnp.bfloat16)[:, :, None, None]).astype(jnp.float32)
    transform = lag_transform().reshape(2 * F, LAGS)
    tiles = masked.reshape(N_BLK, TILE, 3, 2, F)

    def row_tile(row_spectra):
        products = cross_spectra(row_spectra, masked)
        result = jnp.dot(products, transform, precision=lax.Precision.HIGHEST)
        return result.reshape(TILE, N_BLK, TILE, 9, LAGS).astype(jnp.bfloat16)
    stacked = lax.map(row_tile, tiles)
    return stacked.transpose(2, 0, 1, 3, 4, 5).reshape(N_BLK, STATIONS, TILE, 9, LAGS)
```

```python
import functools
import math

import jax
import jax.numpy as jnp
import numpy as np
from jax import lax
from jax.experimental import pallas as pl
from jax.experimental.pallas import tpu as pltpu
from jax.sharding import PartitionSpec as P

F = 320
FIRST = 15
NFFT = 1500
MAXLAG = 64
LAGS = 2 * MAXLAG
LANES = 128
COMPONENTS = 3
ROWS = 8


class Layout:
    def __init__(self, bins, bands):
        self.bins = bins
        self.bands = bands
        self.whole = bins // LANES
        self.rest = bins % LANES
        self.rest_row = 2 * COMPONENTS * self.whole
        self.chunks = 2 * self.whole + 1
        self.depth = bands * self.chunks * LANES
        assert COMPONENTS * self.rest <= LANES and 0 < 2 * self.rest <= LANES
        assert self.rest_row + 2 <= ROWS

    def column(self, band, chunk):
        return (band * self.chunks + chunk) * LANES


def lag_table(layout):
    lag_steps = 2 * np.arange(LAGS, dtype=np.int64) - 2 * MAXLAG + 1
    bins = np.arange(layout.bins * layout.bands, dtype=np.int64) + FIRST
    phases = math.pi / NFFT * ((bins[:, None] * lag_steps[None, :]) % (2 * NFFT))
    cosine = (np.cos(phases) / math.sqrt(F)).astype(np.float32)
    sine = (-np.sin(phases) / math.sqrt(F)).astype(np.float32)
    table = np.zeros((layout.depth, LAGS), np.float32)
    for band in range(layout.bands):
        first = band * layout.bins
        for chunk in range(layout.whole):
            rows = slice(first + chunk * LANES, first + (chunk + 1) * LANES)
            table[layout.column(band, 2 * chunk) :][:LANES] = cosine[rows]
            table[layout.column(band, 2 * chunk + 1) :][:LANES] = sine[rows]
        rows = slice(first + layout.whole * LANES, first + layout.bins)
        start = layout.column(band, 2 * layout.whole)
        table[start : start + layout.rest] = cosine[rows]
        table[start + layout.rest : start + 2 * layout.rest] = sine[rows]
    high = table.astype(jnp.bfloat16)
    low = (table - high.astype(np.float32)).astype(jnp.bfloat16)
    return np.concatenate([high, low], axis=1)


def pack_kernel(layout, copies, quality_ref, spectra_ref, pieces_ref, packed_ref, wide):
    stations = spectra_ref.shape[0]
    wide[...] = jnp.zeros_like(wide)
    lane = lax.broadcasted_iota(jnp.int32, (2, LANES), 1)
    for s in range(stations):
        rests = jnp.zeros((2, LANES), jnp.float32)
        for a in range(COMPONENTS):
            usable = quality_ref[s, a].astype(jnp.float32)
            both = spectra_ref[s, a].astype(jnp.float32) * usable
            for chunk in range(layout.whole):
                row = s * ROWS + 2 * (a * layout.whole + chunk)
                wide[row : row + 2, :] = both[:, chunk * LANES : (chunk + 1) * LANES]
            rest = both[:, layout.whole * LANES :]
            padded = jnp.concatenate([rest, jnp.zeros((2, LANES - layout.rest), jnp.float32)], axis=1)
            rests = rests + (pltpu.roll(padded, a * layout.rest, 1) if a else padded)
        row = s * ROWS + layout.rest_row
        wide[row : row + 2, :] = rests
    for s in range(stations):
        piece = wide[s * ROWS : (s + 1) * ROWS, :].astype(jnp.bfloat16)
        packed_ref[s] = piece
        for copy in range(copies):
            pieces_ref[copy * stations + s] = piece


def correlate_kernel(layout, peers, table_ref, pieces_ref, *rest):
    bands = layout.bands
    own_refs = rest[:bands]
    out_ref, partner, own, high, low, sums = rest[bands:]
    stations = out_ref.shape[1]
    place = lax.axis_index("band")
    partner[...] = pieces_ref[...].astype(jnp.float32).reshape(partner.shape)
    for k in range(bands):
        band = lax.rem(place + k, bands)
        start = pl.multiple_of(band * (stations * ROWS), stations * ROWS)
        own[pl.ds(start, stations * ROWS), :] = (
            own_refs[k][...].astype(jnp.float32).reshape(stations * ROWS, LANES)
        )

    lane = lax.broadcasted_iota(jnp.int32, (1, LANES), 1)
    first_half = lane < layout.rest

    def at_front(rows, component):
        shift = (LANES - component * layout.rest) % LANES
        return pltpu.roll(rows, shift, 1) if shift else rows

    def at_second(rows, component):
        shift = (LANES - (component - 1) * layout.rest) % LANES
        return pltpu.roll(rows, shift, 1) if shift else rows

    def partner_rows(band, row):
        return partner[pl.ds(band * ROWS + row, peers, stride=bands * ROWS), :]

    for band in range(bands):
        real_rest = partner_rows(band, layout.rest_row)
        imag_rest = partner_rows(band, layout.rest_row + 1)
        for b in range(COMPONENTS):
            chunks = []
            for chunk in range(layout.whole):
                row = 2 * (b * layout.whole + chunk)
                chunks.append((partner_rows(band, row), partner_rows(band, row + 1)))
            both_real = jnp.where(first_half, at_front(real_rest, b), at_second(real_rest, b))
            both_imag = jnp.where(first_half, at_front(imag_rest, b), at_second(imag_rest, b))
            for i in range(stations):
                base = (band * stations + i) * ROWS
                for a in range(COMPONENTS):
                    group = ((i * COMPONENTS + a) * COMPONENTS + b) * peers

                    def store(chunk, value):
                        column = layout.column(band, chunk)
                        upper = value.astype(jnp.bfloat16)
                        lower = value - upper.astype(jnp.float32)
                        high[group : group + peers, column : column + LANES] = upper
                        low[group : group + peers, column : column + LANES] = lower.astype(jnp.bfloat16)

                    for chunk in range(layout.whole):
                        row = base + 2 * (a * layout.whole + chunk)
                        x_real = own[row : row + 1, :]
                        x_imag = own[row + 1 : row + 2, :]
                        z_real, z_imag = chunks[chunk]
                        store(2 * chunk, x_real * z_real + x_imag * z_imag)
                        store(2 * chunk + 1, x_imag * z_real - x_real * z_imag)
                    row = base + layout.rest_row
                    x_real = own[row : row + 1, :]
                    x_imag = own[row + 1 : row + 2, :]
                    second = (lane >= layout.rest) & (lane < 2 * layout.rest)
                    zero = jnp.zeros_like(x_real)
                    with_real = jnp.where(
                        first_half, at_front(x_real, a), jnp.where(second, at_second(x_imag, a), zero)
                    )
                    with_imag = jnp.where(
                        first_half, at_front(x_imag, a), jnp.where(second, -at_second(x_real, a), zero)
                    )
                    store(2 * layout.whole, with_real * both_real + with_imag * both_imag)

    result = jnp.dot(high[...], table_ref[...], preferred_element_type=jnp.float32)
    result = (
        result[:, :LAGS]
        + result[:, LAGS:]
        + jnp.dot(low[...], table_ref[:, :LAGS], preferred_element_type=jnp.float32)
    )
    pairs = COMPONENTS * COMPONENTS
    slot = 16
    for i in range(stations):
        for ab in range(pairs):
            group = (i * pairs + ab) * peers
            sums[pl.ds(i * slot + ab, peers, stride=stations * slot), :] = result[group : group + peers]
    for v in range(peers):
        for i in range(stations):
            start = (v * stations + i) * slot
            out_ref[v, i, 0] = sums[start : start + pairs, :].astype(jnp.bfloat16)


def body(spectra, quality):
    stations = spectra.shape[0]
    peers = lax.axis_size("blk")
    bands = lax.axis_size("band")
    assert stations == bands
    layout = Layout(spectra.shape[3], bands)
    vmem = pl.BlockSpec(memory_space=pltpu.VMEM)
    pieces, packed = pl.pallas_call(
        functools.partial(pack_kernel, layout, peers),
        out_shape=(
            jax.ShapeDtypeStruct((peers * bands, ROWS, LANES), jnp.bfloat16),
            jax.ShapeDtypeStruct((stations, ROWS, LANES), jnp.bfloat16),
        ),
        in_specs=[pl.BlockSpec(memory_space=pltpu.SMEM), vmem],
        out_specs=(vmem, vmem),
        scratch_shapes=[pltpu.VMEM((stations * ROWS, LANES), jnp.float32)],
        name="pack",
    )(quality, spectra)
    own = [packed]
    for k in range(1, bands):
        own.append(lax.ppermute(packed, "band", [((i + k) % bands, i) for i in range(bands)]))
    received = lax.all_to_all(pieces, ("blk", "band"), split_axis=0, concat_axis=0, tiled=True)
    rows = stations * COMPONENTS * COMPONENTS * peers
    return pl.pallas_call(
        functools.partial(correlate_kernel, layout, peers),
        out_shape=jax.ShapeDtypeStruct(
            (peers, stations, 1, COMPONENTS * COMPONENTS, LAGS), jnp.bfloat16
        ),
        in_specs=[vmem] * (2 + bands),
        out_specs=vmem,
        scratch_shapes=[
            pltpu.VMEM((peers * bands * ROWS, LANES), jnp.float32),
            pltpu.VMEM((bands * stations * ROWS, LANES), jnp.float32),
            pltpu.VMEM((rows, layout.depth), jnp.bfloat16),
            pltpu.VMEM((rows, layout.depth), jnp.bfloat16),
            pltpu.VMEM((peers * stations * 16, LANES), jnp.float32),
        ],
        compiler_params=pltpu.CompilerParams(vmem_limit_bytes=40 * 1024 * 1024),
        name="correlate",
    )(jnp.asarray(lag_table(layout)), received, *own)


def solution(mesh):
    placed = (P("blk", None, None, "band"), P("blk", None))
    return jax.shard_map(
        body,
        mesh=mesh,
        in_specs=placed,
        out_specs=P(None, "blk", "band", None, None),
        check_vma=False,
    )
```

```python
import functools
import math

import jax
import jax.numpy as jnp
from jax import lax
from jax.experimental import pallas as pl
from jax.experimental.pallas import tpu as pltpu
from jax.sharding import PartitionSpec as P

F = 320
FIRST = 15
NFFT = 1500
MAXLAG = 64
LAGS = 2 * MAXLAG
LANES = 128
COMPONENTS = 3
PAIRS = COMPONENTS * COMPONENTS
ROWS = 8
CORES = 2
VMEM_LIMIT = 40 * 1024 * 1024


class Layout:
    def __init__(self, stations, bins, bands, peers):
        self.stations = stations
        self.bins = bins
        self.bands = bands
        self.peers = peers
        self.halves = peers // CORES
        self.slots = self.halves * bands
        self.whole = bins // LANES
        self.rest = bins % LANES
        self.rest_row = 2 * COMPONENTS * self.whole
        self.chunks = 2 * self.whole + 1
        self.depth = bands * self.chunks * LANES
        self.groups = stations * PAIRS
        self.rows = self.groups * self.halves
        assert stations == bands and stations % 2 == 0 and bins % ROWS == 0
        assert 0 < self.rest and COMPONENTS * self.rest <= LANES
        assert self.rest_row + 2 <= ROWS

    def slot(self, half, band):
        return (half * self.bands + band + 1) % self.slots

    def crossed(self, half):
        return half < self.halves // 2

    def column(self, band, chunk):
        return (band * self.chunks + chunk) * LANES


def pack_kernel(layout, quality_ref, spectra_ref, pieces_ref, wide):
    stations = layout.stations
    if layout.rest_row + 2 < ROWS:
        wide[...] = jnp.zeros_like(wide)
    for s in range(stations):
        rests = jnp.zeros((2, LANES), jnp.float32)
        for a in range(COMPONENTS):
            usable = quality_ref[s, a].astype(jnp.float32)
            both = spectra_ref[s, a].astype(jnp.float32) * usable
            for chunk in range(layout.whole):
                row = s * ROWS + 2 * (a * layout.whole + chunk)
                wide[row : row + 2, :] = both[:, chunk * LANES : (chunk + 1) * LANES]
            rest = both[:, layout.whole * LANES :]
            padded = jnp.concatenate([rest, jnp.zeros((2, LANES - layout.rest), jnp.float32)], axis=1)
            rests = rests + (pltpu.roll(padded, a * layout.rest, 1) if a else padded)
        row = s * ROWS + layout.rest_row
        wide[row : row + 2, :] = rests
    packed = [wide[s * ROWS : (s + 1) * ROWS, :] for s in range(stations)]
    for band in range(layout.bands):
        order = [packed[(band + k) % stations] for k in range(stations)]
        piece = jnp.concatenate(order).astype(jnp.bfloat16)
        for half in range(layout.halves):
            pieces_ref[layout.slot(half, band)] = piece


def at_block(layout, rows, component, block):
    shift = ((block - component) * layout.rest) % LANES
    return pltpu.roll(rows, shift, 1) if shift else rows


def lag_table(layout, anchors, table_ref):
    steps = 2 * lax.broadcasted_iota(jnp.int32, (ROWS, LAGS), 1) - 2 * MAXLAG + 1

    def wave(bins):
        index = lax.rem(bins * steps, 2 * NFFT)
        phases = math.pi / NFFT * index.astype(jnp.float32)
        return jnp.cos(phases), jnp.sin(phases)

    sublane = lax.broadcasted_iota(jnp.int32, (ROWS, LAGS), 0)
    near_cos, near_sin = wave(sublane)
    count = layout.bins * layout.bands // ROWS
    padded = -(-count // ROWS)
    for block in range(padded):
        cosine, sine = wave((sublane + block * ROWS) * ROWS + FIRST)
        anchors[0, block * ROWS : (block + 1) * ROWS, :] = cosine / math.sqrt(F)
        anchors[1, block * ROWS : (block + 1) * ROWS, :] = sine / math.sqrt(F)

    def put(start, values):
        high = values.astype(jnp.bfloat16)
        table_ref[start : start + values.shape[0], :LAGS] = high
        table_ref[start : start + values.shape[0], LAGS:] = (values - high.astype(jnp.float32)).astype(jnp.bfloat16)

    def pair(first, bins):
        cosines, sines = [], []
        for g in range(first // ROWS, (first + bins) // ROWS):
            cosine = anchors[0, g : g + 1, :]
            sine = anchors[1, g : g + 1, :]
            cosines.append(cosine * near_cos - sine * near_sin)
            sines.append(-(sine * near_cos + cosine * near_sin))
        return jnp.concatenate(cosines), jnp.concatenate(sines)

    for band in range(layout.bands):
        first = band * layout.bins
        for chunk in range(layout.whole):
            cosine, sine = pair(first + chunk * LANES, LANES)
            put(layout.column(band, 2 * chunk), cosine)
            put(layout.column(band, 2 * chunk + 1), sine)
        cosine, sine = pair(first + layout.whole * LANES, layout.rest)
        start = layout.column(band, 2 * layout.whole)
        zeros = jnp.zeros((LANES - 2 * layout.rest, LAGS), jnp.float32)
        put(start, jnp.concatenate([cosine, sine, zeros]))


def own_rows(layout, pieces_ref, own, rest_ref):
    stations = layout.stations
    here = lax.div(lax.axis_index("blk"), CORES) * layout.bands
    place = lax.axis_index("band")
    for band in range(layout.bands):
        piece = pieces_ref[lax.rem(here + band + 1, layout.slots)].astype(jnp.float32)
        for k in range(stations):
            start = pl.multiple_of((band * stations + lax.rem(place + k, stations)) * ROWS, ROWS)
            own[pl.ds(start, ROWS), :] = piece[k * ROWS : (k + 1) * ROWS]
    lane = lax.broadcasted_iota(jnp.int32, (1, LANES), 1)
    in_real = lane < layout.rest
    in_imag = (lane >= layout.rest) & (lane < 2 * layout.rest)
    zero = jnp.zeros((1, LANES), jnp.float32)
    for band in range(layout.bands):
        for i in range(stations):
            row = (band * stations + i) * ROWS + layout.rest_row
            real = own[row : row + 1, :]
            imag = own[row + 1 : row + 2, :]
            for a in range(COMPONENTS):
                to = 2 * ((band * stations + i) * COMPONENTS + a)
                rest_ref[to : to + 1, :] = jnp.where(
                    in_real, at_block(layout, real, a, 0), jnp.where(in_imag, at_block(layout, imag, a, 1), zero)
                )
                rest_ref[to + 1 : to + 2, :] = jnp.where(
                    in_real, at_block(layout, imag, a, 0), jnp.where(in_imag, -at_block(layout, real, a, 1), zero)
                )


def correlated(layout, pieces_ref, table_ref, own, rests, partner, high, low):
    for half in range(layout.halves):
        for band in range(layout.bands):
            row = (half * layout.bands + band) * ROWS
            partner[row : row + ROWS, :] = pieces_ref[layout.slot(half, band), :ROWS, :].astype(jnp.float32)

    def partner_rows(band, row):
        return partner[pl.ds(band * ROWS + row, layout.halves, stride=layout.bands * ROWS), :]

    lane = lax.broadcasted_iota(jnp.int32, (1, LANES), 1)
    in_real = lane < layout.rest
    for band in range(layout.bands):
        real_rest = partner_rows(band, layout.rest_row)
        imag_rest = partner_rows(band, layout.rest_row + 1)
        for b in range(COMPONENTS):
            first = 2 * b * layout.whole
            parts = [partner_rows(band, first + k) for k in range(2 * layout.whole)]
            both_real = jnp.where(in_real, at_block(layout, real_rest, b, 0), at_block(layout, real_rest, b, 1))
            both_imag = jnp.where(in_real, at_block(layout, imag_rest, b, 0), at_block(layout, imag_rest, b, 1))
            for a in range(COMPONENTS):
                values = [[] for _ in range(layout.chunks)]
                for i in range(layout.stations):
                    base = (band * layout.stations + i) * ROWS
                    for chunk in range(layout.whole):
                        row = base + 2 * (a * layout.whole + chunk)
                        x_real = own[row : row + 1, :]
                        x_imag = own[row + 1 : row + 2, :]
                        z_real, z_imag = parts[2 * chunk], parts[2 * chunk + 1]
                        values[2 * chunk].append(x_real * z_real + x_imag * z_imag)
                        values[2 * chunk + 1].append(x_imag * z_real - x_real * z_imag)
                    row = 2 * ((band * layout.stations + i) * COMPONENTS + a)
                    values[2 * layout.whole].append(
                        rests[row : row + 1, :] * both_real + rests[row + 1 : row + 2, :] * both_imag
                    )
                start = (b * COMPONENTS + a) * layout.stations * layout.halves
                end = start + layout.stations * layout.halves
                for chunk in range(layout.chunks):
                    value = jnp.concatenate(values[chunk])
                    upper = value.astype(jnp.bfloat16)
                    column = layout.column(band, chunk)
                    high[start:end, column : column + LANES] = upper
                    low[start:end, column : column + LANES] = (value - upper.astype(jnp.float32)).astype(jnp.bfloat16)

    both = jnp.dot(high[...], table_ref[...], preferred_element_type=jnp.float32)
    last = jnp.dot(low[...], table_ref[:, :LAGS], preferred_element_type=jnp.float32)
    return both[:, :LAGS] + (both[:, LAGS:] + last)


def near_kernel(layout, pieces_ref, sums_ref, table_ref, own_ref, rest_ref, partner, high, low, anchors):
    lag_table(layout, anchors, table_ref)
    own_rows(layout, pieces_ref, own_ref, rest_ref)
    sums_ref[...] = correlated(layout, pieces_ref, table_ref, own_ref, rest_ref, partner, high, low)


def far_kernel(layout, pieces_ref, near_ref, table_ref, own_ref, rest_ref, out_ref, partner, high, low, sums):
    far = correlated(layout, pieces_ref, table_ref, own_ref, rest_ref, partner, high, low)
    blk = lax.axis_index("blk")
    core = lax.rem(blk, CORES)
    team = jnp.where(layout.crossed(lax.div(blk, CORES)), 1 - core, core)
    halves = lax.broadcasted_iota(jnp.int32, (layout.halves, LAGS), 0)
    near_first = layout.crossed(halves).astype(jnp.int32) == team
    for b in range(COMPONENTS):
        for a in range(COMPONENTS):
            for i in range(layout.stations):
                group = (b * COMPONENTS + a) * layout.stations + i
                rows = slice(group * layout.halves, (group + 1) * layout.halves)
                for origin in range(CORES):
                    taken = near_first if origin == 0 else jnp.logical_not(near_first)
                    first = origin * layout.groups + (a * COMPONENTS + b) * layout.stations + i
                    to = pl.ds(first, layout.halves, stride=CORES * layout.groups)
                    sums[to, :] = jnp.where(taken, near_ref[rows, :], far[rows])
    out_ref[...] = sums[...].astype(jnp.bfloat16)


def body(spectra, quality):
    peers = lax.axis_size("blk")
    bands = lax.axis_size("band")
    layout = Layout(spectra.shape[0], spectra.shape[3], bands, peers)
    vmem = pl.BlockSpec(memory_space=pltpu.VMEM)
    params = pltpu.CompilerParams(vmem_limit_bytes=VMEM_LIMIT)
    piece_rows = layout.stations * ROWS
    pieces = pl.pallas_call(
        functools.partial(pack_kernel, layout),
        out_shape=pltpu.VMEM((layout.slots, piece_rows, LANES), jnp.bfloat16),
        in_specs=[pl.BlockSpec(memory_space=pltpu.SMEM), vmem],
        out_specs=vmem,
        scratch_shapes=[pltpu.VMEM((piece_rows, LANES), jnp.float32)],
        name="pack",
    )(quality, spectra)
    groups = [[0] * layout.slots for _ in range(CORES)]
    for half in range(layout.halves):
        for core in range(CORES):
            team = 1 - core if layout.crossed(half) else core
            for band in range(bands):
                groups[team][layout.slot(half, band)] = (half * CORES + core) * bands + band
    near = lax.all_to_all(
        pieces, ("blk", "band"), split_axis=0, concat_axis=0, tiled=True, axis_index_groups=groups
    )
    far = lax.ppermute(near, "blk", [(i, i ^ 1) for i in range(peers)])
    work = [
        pltpu.VMEM((layout.slots * ROWS, LANES), jnp.float32),
        pltpu.VMEM((layout.rows, layout.depth), jnp.bfloat16),
        pltpu.VMEM((layout.rows, layout.depth), jnp.bfloat16),
    ]
    kept = pl.pallas_call(
        functools.partial(near_kernel, layout),
        out_shape=(
            pltpu.VMEM((layout.rows, LAGS), jnp.float32),
            pltpu.VMEM((layout.depth, 2 * LAGS), jnp.bfloat16),
            pltpu.VMEM((bands * layout.stations * ROWS, LANES), jnp.float32),
            pltpu.VMEM((2 * bands * layout.stations * COMPONENTS, LANES), jnp.float32),
        ),
        in_specs=[vmem],
        out_specs=(vmem,) * 4,
        scratch_shapes=work
        + [pltpu.VMEM((2, -(-layout.bins * bands // (ROWS * ROWS)) * ROWS, LAGS), jnp.float32)],
        compiler_params=params,
        cost_estimate=pl.CostEstimate(flops=10**8, bytes_accessed=10**6, transcendentals=0),
        name="near",
    )(near)
    result = pl.pallas_call(
        functools.partial(far_kernel, layout),
        out_shape=jax.ShapeDtypeStruct((CORES * layout.rows, LAGS), jnp.bfloat16),
        in_specs=[vmem] * 5,
        out_specs=vmem,
        scratch_shapes=work + [pltpu.VMEM((CORES * layout.rows, LAGS), jnp.float32)],
        compiler_params=params,
        name="far",
    )(far, *kept)
    shape = (peers, 1, PAIRS, layout.stations, LAGS)
    return result.reshape(shape).transpose(0, 3, 1, 2, 4)


def solution(mesh):
    placed = (P("blk", None, None, "band"), P("blk", None))
    return jax.shard_map(
        body,
        mesh=mesh,
        in_specs=placed,
        out_specs=P(None, "blk", "band", None, None),
        check_vma=False,
    )
```

```python
import functools
import math

import jax
import jax.numpy as jnp
from jax import lax
from jax.experimental import pallas as pl
from jax.experimental.pallas import tpu as pltpu
from jax.sharding import PartitionSpec as P

F = 320
FIRST = 15
NFFT = 1500
MAXLAG = 64
LAGS = 2 * MAXLAG
LANES = 128
COMPONENTS = 3
PAIRS = COMPONENTS * COMPONENTS
ROWS = 8
CORES = 2
VMEM_LIMIT = 40 * 1024 * 1024


class Layout:
    def __init__(self, stations, bins, bands, peers):
        self.stations = stations
        self.bins = bins
        self.bands = bands
        self.peers = peers
        self.halves = peers // CORES
        self.slots = self.halves * bands
        self.whole = bins // LANES
        self.rest = bins % LANES
        self.rest_row = 2 * COMPONENTS * self.whole
        self.chunks = 2 * self.whole + 1
        self.depth = bands * self.chunks * LANES
        self.groups = stations * PAIRS
        self.rows = self.groups * self.halves
        assert stations == bands and stations % 2 == 0 and bins % ROWS == 0
        assert 0 < self.rest and COMPONENTS * self.rest <= LANES
        assert self.rest_row + 2 <= ROWS

    def slot(self, half, band):
        return (half * self.bands + band + 1) % self.slots

    def crossed(self, half):
        return half < self.halves // 2

    def column(self, band, chunk):
        return (band * self.chunks + chunk) * LANES


def pack_kernel(layout, quality_ref, spectra_ref, pieces_ref, wide):
    stations = layout.stations
    if layout.rest_row + 2 < ROWS:
        wide[...] = jnp.zeros_like(wide)
    for s in range(stations):
        rests = jnp.zeros((2, LANES), jnp.float32)
        for a in range(COMPONENTS):
            usable = quality_ref[s, a].astype(jnp.float32)
            both = spectra_ref[s, a].astype(jnp.float32) * usable
            for chunk in range(layout.whole):
                row = s * ROWS + 2 * (a * layout.whole + chunk)
                wide[row : row + 2, :] = both[:, chunk * LANES : (chunk + 1) * LANES]
            rest = both[:, layout.whole * LANES :]
            padded = jnp.concatenate([rest, jnp.zeros((2, LANES - layout.rest), jnp.float32)], axis=1)
            rests = rests + (pltpu.roll(padded, a * layout.rest, 1) if a else padded)
        row = s * ROWS + layout.rest_row
        wide[row : row + 2, :] = rests
    packed = [wide[s * ROWS : (s + 1) * ROWS, :] for s in range(stations)]
    for band in range(layout.bands):
        order = [packed[(band + k) % stations] for k in range(stations)]
        piece = jnp.concatenate(order).astype(jnp.bfloat16)
        for half in range(layout.halves):
            pieces_ref[layout.slot(half, band)] = piece


def at_block(layout, rows, component, block):
    shift = ((block - component) * layout.rest) % LANES
    return pltpu.roll(rows, shift, 1) if shift else rows


def lag_table(layout, anchors, table_ref):
    steps = 2 * lax.broadcasted_iota(jnp.int32, (ROWS, LAGS), 1) - 2 * MAXLAG + 1

    def wave(bins):
        index = lax.rem(bins * steps, 2 * NFFT)
        phases = math.pi / NFFT * index.astype(jnp.float32)
        return jnp.cos(phases), jnp.sin(phases)

    sublane = lax.broadcasted_iota(jnp.int32, (ROWS, LAGS), 0)
    near_cos, near_sin = wave(sublane)
    count = layout.bins * layout.bands // ROWS
    padded = -(-count // ROWS)
    for block in range(padded):
        cosine, sine = wave((sublane + block * ROWS) * ROWS + FIRST)
        anchors[0, block * ROWS : (block + 1) * ROWS, :] = cosine / math.sqrt(F)
        anchors[1, block * ROWS : (block + 1) * ROWS, :] = sine / math.sqrt(F)

    def put(start, values):
        high = values.astype(jnp.bfloat16)
        table_ref[start : start + values.shape[0], :LAGS] = high
        table_ref[start : start + values.shape[0], LAGS:] = (values - high.astype(jnp.float32)).astype(jnp.bfloat16)

    def pair(first, bins):
        cosines, sines = [], []
        for g in range(first // ROWS, (first + bins) // ROWS):
            cosine = anchors[0, g : g + 1, :]
            sine = anchors[1, g : g + 1, :]
            cosines.append(cosine * near_cos - sine * near_sin)
            sines.append(-(sine * near_cos + cosine * near_sin))
        return jnp.concatenate(cosines), jnp.concatenate(sines)

    for band in range(layout.bands):
        first = band * layout.bins
        for chunk in range(layout.whole):
            cosine, sine = pair(first + chunk * LANES, LANES)
            put(layout.column(band, 2 * chunk), cosine)
            put(layout.column(band, 2 * chunk + 1), sine)
        cosine, sine = pair(first + layout.whole * LANES, layout.rest)
        start = layout.column(band, 2 * layout.whole)
        zeros = jnp.zeros((LANES - 2 * layout.rest, LAGS), jnp.float32)
        put(start, jnp.concatenate([cosine, sine, zeros]))


def own_rows(layout, pieces_ref, own, rest_ref):
    stations = layout.stations
    here = lax.div(lax.axis_index("blk"), CORES) * layout.bands
    place = lax.axis_index("band")
    for band in range(layout.bands):
        piece = pieces_ref[lax.rem(here + band + 1, layout.slots)].astype(jnp.float32)
        for k in range(stations):
            start = pl.multiple_of((band * stations + lax.rem(place + k, stations)) * ROWS, ROWS)
            own[pl.ds(start, ROWS), :] = piece[k * ROWS : (k + 1) * ROWS]
    lane = lax.broadcasted_iota(jnp.int32, (1, LANES), 1)
    in_real = lane < layout.rest
    in_imag = (lane >= layout.rest) & (lane < 2 * layout.rest)
    zero = jnp.zeros((1, LANES), jnp.float32)
    for band in range(layout.bands):
        for i in range(stations):
            row = (band * stations + i) * ROWS + layout.rest_row
            real = own[row : row + 1, :]
            imag = own[row + 1 : row + 2, :]
            for a in range(COMPONENTS):
                to = 2 * ((band * stations + i) * COMPONENTS + a)
                rest_ref[to : to + 1, :] = jnp.where(
                    in_real, at_block(layout, real, a, 0), jnp.where(in_imag, at_block(layout, imag, a, 1), zero)
                )
                rest_ref[to + 1 : to + 2, :] = jnp.where(
                    in_real, at_block(layout, imag, a, 0), jnp.where(in_imag, -at_block(layout, real, a, 1), zero)
                )


def correlated(layout, pieces_ref, table_ref, own, rests, partner, high, low):
    for half in range(layout.halves):
        for band in range(layout.bands):
            row = (half * layout.bands + band) * ROWS
            partner[row : row + ROWS, :] = pieces_ref[layout.slot(half, band)].astype(jnp.float32)[:ROWS]

    def partner_rows(band, row):
        return partner[pl.ds(band * ROWS + row, layout.halves, stride=layout.bands * ROWS), :]

    lane = lax.broadcasted_iota(jnp.int32, (1, LANES), 1)
    in_real = lane < layout.rest
    for band in range(layout.bands):
        real_rest = partner_rows(band, layout.rest_row)
        imag_rest = partner_rows(band, layout.rest_row + 1)
        for b in range(COMPONENTS):
            first = 2 * b * layout.whole
            parts = [partner_rows(band, first + k) for k in range(2 * layout.whole)]
            both_real = jnp.where(in_real, at_block(layout, real_rest, b, 0), at_block(layout, real_rest, b, 1))
            both_imag = jnp.where(in_real, at_block(layout, imag_rest, b, 0), at_block(layout, imag_rest, b, 1))
            for a in range(COMPONENTS):
                values = [[] for _ in range(layout.chunks)]
                for i in range(layout.stations):
                    base = (band * layout.stations + i) * ROWS
                    for chunk in range(layout.whole):
                        row = base + 2 * (a * layout.whole + chunk)
                        x_real = own[row : row + 1, :]
                        x_imag = own[row + 1 : row + 2, :]
                        z_real, z_imag = parts[2 * chunk], parts[2 * chunk + 1]
                        values[2 * chunk].append(x_real * z_real + x_imag * z_imag)
                        values[2 * chunk + 1].append(x_imag * z_real - x_real * z_imag)
                    row = 2 * ((band * layout.stations + i) * COMPONENTS + a)
                    values[2 * layout.whole].append(
                        rests[row : row + 1, :] * both_real + rests[row + 1 : row + 2, :] * both_imag
                    )
                start = (b * COMPONENTS + a) * layout.stations * layout.halves
                end = start + layout.stations * layout.halves
                for chunk in range(layout.chunks):
                    value = jnp.concatenate(values[chunk])
                    upper = value.astype(jnp.bfloat16)
                    column = layout.column(band, chunk)
                    high[start:end, column : column + LANES] = upper
                    low[start:end, column : column + LANES] = (value - upper.astype(jnp.float32)).astype(jnp.bfloat16)

    both = jnp.dot(high[...], table_ref[...], preferred_element_type=jnp.float32)
    last = jnp.dot(low[...], table_ref[:, :LAGS], preferred_element_type=jnp.float32)
    return both[:, :LAGS] + (both[:, LAGS:] + last)


def near_kernel(layout, pieces_ref, sums_ref, table_ref, own_ref, rest_ref, partner, high, low, anchors):
    lag_table(layout, anchors, table_ref)
    own_rows(layout, pieces_ref, own_ref, rest_ref)
    sums_ref[...] = correlated(layout, pieces_ref, table_ref, own_ref, rest_ref, partner, high, low)


def far_kernel(layout, pieces_ref, near_ref, table_ref, own_ref, rest_ref, out_ref, partner, high, low, sums):
    far = correlated(layout, pieces_ref, table_ref, own_ref, rest_ref, partner, high, low)
    blk = lax.axis_index("blk")
    core = lax.rem(blk, CORES)
    team = jnp.where(layout.crossed(lax.div(blk, CORES)), 1 - core, core)
    halves = lax.broadcasted_iota(jnp.int32, (layout.halves, LAGS), 0)
    near_first = layout.crossed(halves).astype(jnp.int32) == team
    for b in range(COMPONENTS):
        for a in range(COMPONENTS):
            for i in range(layout.stations):
                group = (b * COMPONENTS + a) * layout.stations + i
                rows = slice(group * layout.halves, (group + 1) * layout.halves)
                for origin in range(CORES):
                    taken = near_first if origin == 0 else jnp.logical_not(near_first)
                    first = origin * layout.groups + (a * COMPONENTS + b) * layout.stations + i
                    to = pl.ds(first, layout.halves, stride=CORES * layout.groups)
                    sums[to, :] = jnp.where(taken, near_ref[rows, :], far[rows])
    out_ref[...] = sums[...].astype(jnp.bfloat16)


def body(spectra, quality):
    peers = lax.axis_size("blk")
    bands = lax.axis_size("band")
    layout = Layout(spectra.shape[0], spectra.shape[3], bands, peers)
    vmem = pl.BlockSpec(memory_space=pltpu.VMEM)
    params = pltpu.CompilerParams(vmem_limit_bytes=VMEM_LIMIT)
    piece_rows = layout.stations * ROWS
    pieces = pl.pallas_call(
        functools.partial(pack_kernel, layout),
        out_shape=pltpu.VMEM((layout.slots, piece_rows, LANES), jnp.bfloat16),
        in_specs=[pl.BlockSpec(memory_space=pltpu.SMEM), vmem],
        out_specs=vmem,
        scratch_shapes=[pltpu.VMEM((piece_rows, LANES), jnp.float32)],
        name="pack",
    )(quality, spectra)
    groups = [[0] * layout.slots for _ in range(CORES)]
    for half in range(layout.halves):
        for core in range(CORES):
            team = 1 - core if layout.crossed(half) else core
            for band in range(bands):
                groups[team][layout.slot(half, band)] = (half * CORES + core) * bands + band
    near = lax.all_to_all(
        pieces, ("blk", "band"), split_axis=0, concat_axis=0, tiled=True, axis_index_groups=groups
    )
    far = lax.ppermute(near, "blk", [(i, i ^ 1) for i in range(peers)])
    work = [
        pltpu.VMEM((layout.slots * ROWS, LANES), jnp.float32),
        pltpu.VMEM((layout.rows, layout.depth), jnp.bfloat16),
        pltpu.VMEM((layout.rows, layout.depth), jnp.bfloat16),
    ]
    kept = pl.pallas_call(
        functools.partial(near_kernel, layout),
        out_shape=(
            pltpu.VMEM((layout.rows, LAGS), jnp.float32),
            pltpu.VMEM((layout.depth, 2 * LAGS), jnp.bfloat16),
            pltpu.VMEM((bands * layout.stations * ROWS, LANES), jnp.float32),
            pltpu.VMEM((2 * bands * layout.stations * COMPONENTS, LANES), jnp.float32),
        ),
        in_specs=[vmem],
        out_specs=(vmem,) * 4,
        scratch_shapes=work
        + [pltpu.VMEM((2, -(-layout.bins * bands // (ROWS * ROWS)) * ROWS, LAGS), jnp.float32)],
        compiler_params=params,
        cost_estimate=pl.CostEstimate(flops=10**8, bytes_accessed=10**6, transcendentals=0),
        name="near",
    )(near)
    result = pl.pallas_call(
        functools.partial(far_kernel, layout),
        out_shape=jax.ShapeDtypeStruct((CORES * layout.rows, LAGS), jnp.bfloat16),
        in_specs=[vmem] * 5,
        out_specs=vmem,
        scratch_shapes=work + [pltpu.VMEM((CORES * layout.rows, LAGS), jnp.float32)],
        compiler_params=params,
        name="far",
    )(far, *kept)
    shape = (peers, 1, PAIRS, layout.stations, LAGS)
    return result.reshape(shape).transpose(0, 3, 1, 2, 4)


def solution(mesh):
    placed = (P("blk", None, None, "band"), P("blk", None))
    return jax.shard_map(
        body,
        mesh=mesh,
        in_specs=placed,
        out_specs=P(None, "blk", "band", None, None),
        check_vma=False,
    )
```

```python
import functools
import math

import jax
import jax.numpy as jnp
from jax import lax
from jax.experimental import pallas as pl
from jax.experimental.pallas import tpu as pltpu
from jax.sharding import PartitionSpec as P

F = 320
FIRST = 15
NFFT = 1500
MAXLAG = 64
LAGS = 2 * MAXLAG
LANES = 128
COMPONENTS = 3
PAIRS = COMPONENTS * COMPONENTS
ROWS = 8
CORES = 2
VMEM_LIMIT = 40 * 1024 * 1024


class Layout:
    def __init__(self, stations, bins, bands, peers):
        self.stations = stations
        self.bins = bins
        self.bands = bands
        self.peers = peers
        self.halves = peers // CORES
        self.slots = self.halves * bands
        self.whole = bins // LANES
        self.rest = bins % LANES
        self.rest_row = 2 * COMPONENTS * self.whole
        self.chunks = 2 * self.whole + 1
        self.depth = bands * self.chunks * LANES
        self.groups = stations * PAIRS
        self.rows = self.groups * self.halves
        assert stations == bands and stations % 2 == 0 and bins % ROWS == 0
        assert 0 < self.rest and COMPONENTS * self.rest <= LANES
        assert self.rest_row + 2 <= ROWS

    def slot(self, half, band):
        return (half * self.bands + band + 1) % self.slots

    def crossed(self, half):
        return half < self.halves // 2

    def column(self, band, chunk):
        return (band * self.chunks + chunk) * LANES


def pack_kernel(layout, quality_ref, spectra_ref, pieces_ref, wide):
    stations = layout.stations
    if layout.rest_row + 2 < ROWS:
        wide[...] = jnp.zeros_like(wide)
    for s in range(stations):
        rests = jnp.zeros((2, LANES), jnp.float32)
        for a in range(COMPONENTS):
            usable = quality_ref[s, a].astype(jnp.float32)
            both = spectra_ref[s, a].astype(jnp.float32) * usable
            for chunk in range(layout.whole):
                row = s * ROWS + 2 * (a * layout.whole + chunk)
                wide[row : row + 2, :] = both[:, chunk * LANES : (chunk + 1) * LANES]
            rest = both[:, layout.whole * LANES :]
            padded = jnp.concatenate([rest, jnp.zeros((2, LANES - layout.rest), jnp.float32)], axis=1)
            rests = rests + (pltpu.roll(padded, a * layout.rest, 1) if a else padded)
        row = s * ROWS + layout.rest_row
        wide[row : row + 2, :] = rests
    packed = [wide[s * ROWS : (s + 1) * ROWS, :] for s in range(stations)]
    for band in range(layout.bands):
        order = [packed[(band + k) % stations] for k in range(stations)]
        piece = jnp.concatenate(order).astype(jnp.bfloat16)
        for half in range(layout.halves):
            pieces_ref[layout.slot(half, band)] = piece


def at_block(layout, rows, component, block):
    shift = ((block - component) * layout.rest) % LANES
    return pltpu.roll(rows, shift, 1) if shift else rows


def lag_table(layout, anchors, table_ref):
    steps = 2 * lax.broadcasted_iota(jnp.int32, (ROWS, LAGS), 1) - 2 * MAXLAG + 1

    def wave(bins):
        index = lax.rem(bins * steps, 2 * NFFT)
        phases = math.pi / NFFT * index.astype(jnp.float32)
        return jnp.cos(phases), jnp.sin(phases)

    sublane = lax.broadcasted_iota(jnp.int32, (ROWS, LAGS), 0)
    near_cos, near_sin = wave(sublane)
    count = layout.bins * layout.bands // ROWS
    padded = -(-count // ROWS)
    for block in range(padded):
        cosine, sine = wave((sublane + block * ROWS) * ROWS + FIRST)
        anchors[0, block * ROWS : (block + 1) * ROWS, :] = cosine / math.sqrt(F)
        anchors[1, block * ROWS : (block + 1) * ROWS, :] = sine / math.sqrt(F)

    def put(start, values):
        high = values.astype(jnp.bfloat16)
        table_ref[start : start + values.shape[0], :LAGS] = high
        table_ref[start : start + values.shape[0], LAGS:] = (values - high.astype(jnp.float32)).astype(jnp.bfloat16)

    def pair(first, bins):
        cosines, sines = [], []
        for g in range(first // ROWS, (first + bins) // ROWS):
            cosine = anchors[0, g : g + 1, :]
            sine = anchors[1, g : g + 1, :]
            cosines.append(cosine * near_cos - sine * near_sin)
            sines.append(-(sine * near_cos + cosine * near_sin))
        return jnp.concatenate(cosines), jnp.concatenate(sines)

    for band in range(layout.bands):
        first = band * layout.bins
        for chunk in range(layout.whole):
            cosine, sine = pair(first + chunk * LANES, LANES)
            put(layout.column(band, 2 * chunk), cosine)
            put(layout.column(band, 2 * chunk + 1), sine)
        cosine, sine = pair(first + layout.whole * LANES, layout.rest)
        start = layout.column(band, 2 * layout.whole)
        zeros = jnp.zeros((LANES - 2 * layout.rest, LAGS), jnp.float32)
        put(start, jnp.concatenate([cosine, sine, zeros]))


def own_rows(layout, pieces_ref, own, rest_ref):
    stations = layout.stations
    here = lax.div(lax.axis_index("blk"), CORES) * layout.bands
    place = lax.axis_index("band")
    for band in range(layout.bands):
        piece = pieces_ref[lax.rem(here + band + 1, layout.slots)].astype(jnp.float32)
        for k in range(stations):
            start = pl.multiple_of((band * stations + lax.rem(place + k, stations)) * ROWS, ROWS)
            own[pl.ds(start, ROWS), :] = piece[k * ROWS : (k + 1) * ROWS]
    lane = lax.broadcasted_iota(jnp.int32, (1, LANES), 1)
    in_real = lane < layout.rest
    in_imag = (lane >= layout.rest) & (lane < 2 * layout.rest)
    zero = jnp.zeros((1, LANES), jnp.float32)
    for band in range(layout.bands):
        for i in range(stations):
            row = (band * stations + i) * ROWS + layout.rest_row
            real = own[row : row + 1, :]
            imag = own[row + 1 : row + 2, :]
            for a in range(COMPONENTS):
                to = 2 * ((band * stations + i) * COMPONENTS + a)
                rest_ref[to : to + 1, :] = jnp.where(
                    in_real, at_block(layout, real, a, 0), jnp.where(in_imag, at_block(layout, imag, a, 1), zero)
                )
                rest_ref[to + 1 : to + 2, :] = jnp.where(
                    in_real, at_block(layout, imag, a, 0), jnp.where(in_imag, -at_block(layout, real, a, 1), zero)
                )


def correlated(layout, pieces_ref, table_ref, own, rests, partner):
    for half in range(layout.halves):
        for band in range(layout.bands):
            row = (half * layout.bands + band) * ROWS
            partner[row : row + ROWS, :] = pieces_ref[layout.slot(half, band)].astype(jnp.float32)[:ROWS]

    def partner_rows(band, row):
        return partner[pl.ds(band * ROWS + row, layout.halves, stride=layout.bands * ROWS), :]

    lane = lax.broadcasted_iota(jnp.int32, (1, LANES), 1)
    in_real = lane < layout.rest
    uppers, lowers = [], []
    for band in range(layout.bands):
        real_rest = partner_rows(band, layout.rest_row)
        imag_rest = partner_rows(band, layout.rest_row + 1)
        columns = [[] for _ in range(layout.chunks)]
        for b in range(COMPONENTS):
            first = 2 * b * layout.whole
            parts = [partner_rows(band, first + k) for k in range(2 * layout.whole)]
            both_real = jnp.where(in_real, at_block(layout, real_rest, b, 0), at_block(layout, real_rest, b, 1))
            both_imag = jnp.where(in_real, at_block(layout, imag_rest, b, 0), at_block(layout, imag_rest, b, 1))
            for a in range(COMPONENTS):
                for i in range(layout.stations):
                    base = (band * layout.stations + i) * ROWS
                    for chunk in range(layout.whole):
                        row = base + 2 * (a * layout.whole + chunk)
                        x_real = own[row : row + 1, :]
                        x_imag = own[row + 1 : row + 2, :]
                        z_real, z_imag = parts[2 * chunk], parts[2 * chunk + 1]
                        columns[2 * chunk].append(x_real * z_real + x_imag * z_imag)
                        columns[2 * chunk + 1].append(x_imag * z_real - x_real * z_imag)
                    row = 2 * ((band * layout.stations + i) * COMPONENTS + a)
                    columns[2 * layout.whole].append(
                        rests[row : row + 1, :] * both_real + rests[row + 1 : row + 2, :] * both_imag
                    )
        values = jnp.concatenate([jnp.concatenate(column) for column in columns], axis=1)
        upper = values.astype(jnp.bfloat16)
        lower = (values - upper.astype(jnp.float32)).astype(jnp.bfloat16)
        uppers.append(upper)
        lowers.append(lower)
    both = jnp.dot(jnp.concatenate(uppers, axis=1), table_ref[...], preferred_element_type=jnp.float32)
    last = jnp.dot(jnp.concatenate(lowers, axis=1), table_ref[:, :LAGS], preferred_element_type=jnp.float32)
    return both[:, :LAGS] + (both[:, LAGS:] + last)


def near_kernel(layout, pieces_ref, sums_ref, table_ref, own_ref, rest_ref, partner, anchors):
    lag_table(layout, anchors, table_ref)
    own_rows(layout, pieces_ref, own_ref, rest_ref)
    sums_ref[...] = correlated(layout, pieces_ref, table_ref, own_ref, rest_ref, partner)


def far_kernel(layout, pieces_ref, near_ref, table_ref, own_ref, rest_ref, out_ref, partner, sums):
    far = correlated(layout, pieces_ref, table_ref, own_ref, rest_ref, partner)
    blk = lax.axis_index("blk")
    core = lax.rem(blk, CORES)
    team = jnp.where(layout.crossed(lax.div(blk, CORES)), 1 - core, core)
    halves = lax.broadcasted_iota(jnp.int32, (layout.halves, LAGS), 0)
    near_first = layout.crossed(halves).astype(jnp.int32) == team
    for b in range(COMPONENTS):
        for a in range(COMPONENTS):
            for i in range(layout.stations):
                group = (b * COMPONENTS + a) * layout.stations + i
                rows = slice(group * layout.halves, (group + 1) * layout.halves)
                for origin in range(CORES):
                    taken = near_first if origin == 0 else jnp.logical_not(near_first)
                    first = origin * layout.groups + (a * COMPONENTS + b) * layout.stations + i
                    to = pl.ds(first, layout.halves, stride=CORES * layout.groups)
                    sums[to, :] = jnp.where(taken, near_ref[rows, :], far[rows])
    out_ref[...] = sums[...].astype(jnp.bfloat16)


def body(spectra, quality):
    peers = lax.axis_size("blk")
    bands = lax.axis_size("band")
    layout = Layout(spectra.shape[0], spectra.shape[3], bands, peers)
    vmem = pl.BlockSpec(memory_space=pltpu.VMEM)
    params = pltpu.CompilerParams(vmem_limit_bytes=VMEM_LIMIT)
    piece_rows = layout.stations * ROWS
    pieces = pl.pallas_call(
        functools.partial(pack_kernel, layout),
        out_shape=pltpu.VMEM((layout.slots, piece_rows, LANES), jnp.bfloat16),
        in_specs=[pl.BlockSpec(memory_space=pltpu.SMEM), vmem],
        out_specs=vmem,
        scratch_shapes=[pltpu.VMEM((piece_rows, LANES), jnp.float32)],
        name="pack",
    )(quality, spectra)
    groups = [[0] * layout.slots for _ in range(CORES)]
    for half in range(layout.halves):
        for core in range(CORES):
            team = 1 - core if layout.crossed(half) else core
            for band in range(bands):
                groups[team][layout.slot(half, band)] = (half * CORES + core) * bands + band
    near = lax.all_to_all(
        pieces, ("blk", "band"), split_axis=0, concat_axis=0, tiled=True, axis_index_groups=groups
    )
    far = lax.ppermute(near, "blk", [(i, i ^ 1) for i in range(peers)])
    partner = pltpu.VMEM((layout.slots * ROWS, LANES), jnp.float32)
    kept = pl.pallas_call(
        functools.partial(near_kernel, layout),
        out_shape=(
            pltpu.VMEM((layout.rows, LAGS), jnp.float32),
            pltpu.VMEM((layout.depth, 2 * LAGS), jnp.bfloat16),
            pltpu.VMEM((bands * layout.stations * ROWS, LANES), jnp.float32),
            pltpu.VMEM((2 * bands * layout.stations * COMPONENTS, LANES), jnp.float32),
        ),
        in_specs=[vmem],
        out_specs=(vmem,) * 4,
        scratch_shapes=[
            partner,
            pltpu.VMEM((2, -(-layout.bins * bands // (ROWS * ROWS)) * ROWS, LAGS), jnp.float32),
        ],
        compiler_params=params,
        cost_estimate=pl.CostEstimate(flops=10**8, bytes_accessed=10**6, transcendentals=0),
        name="near",
    )(near)
    result = pl.pallas_call(
        functools.partial(far_kernel, layout),
        out_shape=jax.ShapeDtypeStruct((CORES * layout.rows, LAGS), jnp.bfloat16),
        in_specs=[vmem] * 5,
        out_specs=vmem,
        scratch_shapes=[partner, pltpu.VMEM((CORES * layout.rows, LAGS), jnp.float32)],
        compiler_params=params,
        name="far",
    )(far, *kept)
    shape = (peers, 1, PAIRS, layout.stations, LAGS)
    return result.reshape(shape).transpose(0, 3, 1, 2, 4)


def solution(mesh):
    placed = (P("blk", None, None, "band"), P("blk", None))
    return jax.shard_map(
        body,
        mesh=mesh,
        in_specs=placed,
        out_specs=P(None, "blk", "band", None, None),
        check_vma=False,
    )
```

```python
import functools
import math

import jax
import jax.numpy as jnp
from jax import lax
from jax.experimental import pallas as pl
from jax.experimental.pallas import tpu as pltpu
from jax.sharding import PartitionSpec as P

F = 320
FIRST = 15
NFFT = 1500
MAXLAG = 64
LAGS = 2 * MAXLAG
LANES = 128
COMPONENTS = 3
PAIRS = COMPONENTS * COMPONENTS
ROWS = 8
CORES = 2
VMEM_LIMIT = 40 * 1024 * 1024


class Layout:
    def __init__(self, stations, bins, bands, peers):
        self.stations = stations
        self.bins = bins
        self.bands = bands
        self.peers = peers
        self.halves = peers // CORES
        self.slots = self.halves * bands
        self.whole = bins // LANES
        self.rest = bins % LANES
        self.rest_row = 2 * COMPONENTS * self.whole
        self.chunks = 2 * self.whole + 1
        self.depth = bands * self.chunks * LANES
        self.groups = stations * PAIRS
        self.rows = self.groups * self.halves
        assert stations == bands and stations % 2 == 0 and bins % ROWS == 0
        assert 0 < self.rest and COMPONENTS * self.rest <= LANES
        assert self.rest_row + 2 <= ROWS

    def slot(self, half, band):
        return (half * self.bands + band + 1) % self.slots

    def crossed(self, half):
        return half < self.halves // 2

    def column(self, band, chunk):
        whole = self.chunks - 1
        place = band * whole + chunk if chunk < whole else self.bands * whole + band
        return place * LANES


def pack_kernel(layout, quality_ref, spectra_ref, pieces_ref, wide):
    stations = layout.stations
    if layout.rest_row + 2 < ROWS:
        wide[...] = jnp.zeros_like(wide)
    for s in range(stations):
        rests = jnp.zeros((2, LANES), jnp.float32)
        for a in range(COMPONENTS):
            usable = quality_ref[s, a].astype(jnp.float32)
            both = spectra_ref[s, a].astype(jnp.float32) * usable
            for chunk in range(layout.whole):
                row = s * ROWS + 2 * (a * layout.whole + chunk)
                wide[row : row + 2, :] = both[:, chunk * LANES : (chunk + 1) * LANES]
            rest = both[:, layout.whole * LANES :]
            padded = jnp.concatenate([rest, jnp.zeros((2, LANES - layout.rest), jnp.float32)], axis=1)
            rests = rests + (pltpu.roll(padded, a * layout.rest, 1) if a else padded)
        row = s * ROWS + layout.rest_row
        wide[row : row + 2, :] = rests
    packed = [wide[s * ROWS : (s + 1) * ROWS, :] for s in range(stations)]
    for band in range(layout.bands):
        order = [packed[(band + k) % stations] for k in range(stations)]
        piece = jnp.concatenate(order).astype(jnp.bfloat16)
        for half in range(layout.halves):
            pieces_ref[layout.slot(half, band)] = piece


def at_block(layout, rows, component, block):
    shift = ((block - component) * layout.rest) % LANES
    return pltpu.roll(rows, shift, 1) if shift else rows


def lag_table(layout, anchors, table_ref):
    steps = 2 * lax.broadcasted_iota(jnp.int32, (ROWS, LAGS), 1) - 2 * MAXLAG + 1

    def wave(bins):
        index = lax.rem(bins * steps, 2 * NFFT)
        phases = math.pi / NFFT * index.astype(jnp.float32)
        return jnp.cos(phases), jnp.sin(phases)

    sublane = lax.broadcasted_iota(jnp.int32, (ROWS, LAGS), 0)
    near_cos, near_sin = wave(sublane)
    count = layout.bins * layout.bands // ROWS
    padded = -(-count // ROWS)
    for block in range(padded):
        cosine, sine = wave((sublane + block * ROWS) * ROWS + FIRST)
        anchors[0, block * ROWS : (block + 1) * ROWS, :] = cosine / math.sqrt(F)
        anchors[1, block * ROWS : (block + 1) * ROWS, :] = sine / math.sqrt(F)

    def put(start, values):
        high = values.astype(jnp.bfloat16)
        table_ref[start : start + values.shape[0], :LAGS] = high
        table_ref[start : start + values.shape[0], LAGS:] = (values - high.astype(jnp.float32)).astype(jnp.bfloat16)

    def pair(first, bins):
        cosines, sines = [], []
        for g in range(first // ROWS, (first + bins) // ROWS):
            cosine = anchors[0, g : g + 1, :]
            sine = anchors[1, g : g + 1, :]
            cosines.append(cosine * near_cos - sine * near_sin)
            sines.append(-(sine * near_cos + cosine * near_sin))
        return jnp.concatenate(cosines), jnp.concatenate(sines)

    for band in range(layout.bands):
        first = band * layout.bins
        for chunk in range(layout.whole):
            cosine, sine = pair(first + chunk * LANES, LANES)
            put(layout.column(band, 2 * chunk), cosine)
            put(layout.column(band, 2 * chunk + 1), sine)
        cosine, sine = pair(first + layout.whole * LANES, layout.rest)
        start = layout.column(band, 2 * layout.whole)
        zeros = jnp.zeros((LANES - 2 * layout.rest, LAGS), jnp.float32)
        put(start, jnp.concatenate([cosine, sine, zeros]))


def own_rows(layout, pieces_ref, own, rest_ref):
    stations = layout.stations
    here = lax.div(lax.axis_index("blk"), CORES) * layout.bands
    place = lax.axis_index("band")
    for band in range(layout.bands):
        piece = pieces_ref[lax.rem(here + band + 1, layout.slots)].astype(jnp.float32)
        for k in range(stations):
            start = pl.multiple_of((band * stations + lax.rem(place + k, stations)) * ROWS, ROWS)
            own[pl.ds(start, ROWS), :] = piece[k * ROWS : (k + 1) * ROWS]
    lane = lax.broadcasted_iota(jnp.int32, (1, LANES), 1)
    in_real = lane < layout.rest
    in_imag = (lane >= layout.rest) & (lane < 2 * layout.rest)
    zero = jnp.zeros((1, LANES), jnp.float32)
    for band in range(layout.bands):
        for i in range(stations):
            row = (band * stations + i) * ROWS + layout.rest_row
            real = own[row : row + 1, :]
            imag = own[row + 1 : row + 2, :]
            for a in range(COMPONENTS):
                to = 2 * ((band * stations + i) * COMPONENTS + a)
                rest_ref[to : to + 1, :] = jnp.where(
                    in_real, at_block(layout, real, a, 0), jnp.where(in_imag, at_block(layout, imag, a, 1), zero)
                )
                rest_ref[to + 1 : to + 2, :] = jnp.where(
                    in_real, at_block(layout, imag, a, 0), jnp.where(in_imag, -at_block(layout, real, a, 1), zero)
                )


def correlated(layout, pieces_ref, table_ref, own, rests, partner):
    for half in range(layout.halves):
        for band in range(layout.bands):
            row = (half * layout.bands + band) * ROWS
            partner[row : row + ROWS, :] = pieces_ref[layout.slot(half, band)].astype(jnp.float32)[:ROWS]

    def partner_rows(band, row):
        return partner[pl.ds(band * ROWS + row, layout.halves, stride=layout.bands * ROWS), :]

    lane = lax.broadcasted_iota(jnp.int32, (1, LANES), 1)
    in_real = lane < layout.rest
    values = {}
    for band in range(layout.bands):
        real_rest = partner_rows(band, layout.rest_row)
        imag_rest = partner_rows(band, layout.rest_row + 1)
        columns = [[] for _ in range(layout.chunks)]
        for b in range(COMPONENTS):
            first = 2 * b * layout.whole
            parts = [partner_rows(band, first + k) for k in range(2 * layout.whole)]
            both_real = jnp.where(in_real, at_block(layout, real_rest, b, 0), at_block(layout, real_rest, b, 1))
            both_imag = jnp.where(in_real, at_block(layout, imag_rest, b, 0), at_block(layout, imag_rest, b, 1))
            for a in range(COMPONENTS):
                for i in range(layout.stations):
                    base = (band * layout.stations + i) * ROWS
                    for chunk in range(layout.whole):
                        row = base + 2 * (a * layout.whole + chunk)
                        x_real = own[row : row + 1, :]
                        x_imag = own[row + 1 : row + 2, :]
                        z_real, z_imag = parts[2 * chunk], parts[2 * chunk + 1]
                        columns[2 * chunk].append(x_real * z_real + x_imag * z_imag)
                        columns[2 * chunk + 1].append(x_imag * z_real - x_real * z_imag)
                    row = 2 * ((band * layout.stations + i) * COMPONENTS + a)
                    columns[2 * layout.whole].append(
                        rests[row : row + 1, :] * both_real + rests[row + 1 : row + 2, :] * both_imag
                    )
        for chunk in range(layout.chunks):
            values[layout.column(band, chunk)] = jnp.concatenate(columns[chunk])
    values = [values[column] for column in sorted(values)]
    uppers = [value.astype(jnp.bfloat16) for value in values]
    lowers = [(value - upper.astype(jnp.float32)).astype(jnp.bfloat16) for value, upper in zip(values, uppers)]
    both = jnp.dot(jnp.concatenate(uppers, axis=1), table_ref[...], preferred_element_type=jnp.float32)
    last = jnp.dot(jnp.concatenate(lowers, axis=1), table_ref[:, :LAGS], preferred_element_type=jnp.float32)
    return both[:, :LAGS] + (both[:, LAGS:] + last)


def near_kernel(layout, pieces_ref, sums_ref, table_ref, own_ref, rest_ref, partner, anchors):
    lag_table(layout, anchors, table_ref)
    own_rows(layout, pieces_ref, own_ref, rest_ref)
    sums_ref[...] = correlated(layout, pieces_ref, table_ref, own_ref, rest_ref, partner)


def far_kernel(layout, pieces_ref, near_ref, table_ref, own_ref, rest_ref, out_ref, partner, sums):
    far = correlated(layout, pieces_ref, table_ref, own_ref, rest_ref, partner)
    blk = lax.axis_index("blk")
    core = lax.rem(blk, CORES)
    team = jnp.where(layout.crossed(lax.div(blk, CORES)), 1 - core, core)
    halves = lax.broadcasted_iota(jnp.int32, (layout.halves, LAGS), 0)
    near_first = layout.crossed(halves).astype(jnp.int32) == team
    for b in range(COMPONENTS):
        for a in range(COMPONENTS):
            for i in range(layout.stations):
                group = (b * COMPONENTS + a) * layout.stations + i
                rows = slice(group * layout.halves, (group + 1) * layout.halves)
                for origin in range(CORES):
                    taken = near_first if origin == 0 else jnp.logical_not(near_first)
                    first = origin * layout.groups + (a * COMPONENTS + b) * layout.stations + i
                    to = pl.ds(first, layout.halves, stride=CORES * layout.groups)
                    sums[to, :] = jnp.where(taken, near_ref[rows, :], far[rows])
    out_ref[...] = sums[...].astype(jnp.bfloat16)


def body(spectra, quality):
    peers = lax.axis_size("blk")
    bands = lax.axis_size("band")
    layout = Layout(spectra.shape[0], spectra.shape[3], bands, peers)
    vmem = pl.BlockSpec(memory_space=pltpu.VMEM)
    params = pltpu.CompilerParams(vmem_limit_bytes=VMEM_LIMIT)
    piece_rows = layout.stations * ROWS
    pieces = pl.pallas_call(
        functools.partial(pack_kernel, layout),
        out_shape=pltpu.VMEM((layout.slots, piece_rows, LANES), jnp.bfloat16),
        in_specs=[pl.BlockSpec(memory_space=pltpu.SMEM), vmem],
        out_specs=vmem,
        scratch_shapes=[pltpu.VMEM((piece_rows, LANES), jnp.float32)],
        name="pack",
    )(quality, spectra)
    groups = [[0] * layout.slots for _ in range(CORES)]
    for half in range(layout.halves):
        for core in range(CORES):
            team = 1 - core if layout.crossed(half) else core
            for band in range(bands):
                groups[team][layout.slot(half, band)] = (half * CORES + core) * bands + band
    near = lax.all_to_all(
        pieces, ("blk", "band"), split_axis=0, concat_axis=0, tiled=True, axis_index_groups=groups
    )
    far = lax.ppermute(near[:, :ROWS], "blk", [(i, i ^ 1) for i in range(peers)])
    partner = pltpu.VMEM((layout.slots * ROWS, LANES), jnp.float32)
    kept = pl.pallas_call(
        functools.partial(near_kernel, layout),
        out_shape=(
            pltpu.VMEM((layout.rows, LAGS), jnp.float32),
            pltpu.VMEM((layout.depth, 2 * LAGS), jnp.bfloat16),
            pltpu.VMEM((bands * layout.stations * ROWS, LANES), jnp.float32),
            pltpu.VMEM((2 * bands * layout.stations * COMPONENTS, LANES), jnp.float32),
        ),
        in_specs=[vmem],
        out_specs=(vmem,) * 4,
        scratch_shapes=[
            partner,
            pltpu.VMEM((2, -(-layout.bins * bands // (ROWS * ROWS)) * ROWS, LAGS), jnp.float32),
        ],
        compiler_params=params,
        cost_estimate=pl.CostEstimate(flops=10**8, bytes_accessed=10**6, transcendentals=0),
        name="near",
    )(near)
    result = pl.pallas_call(
        functools.partial(far_kernel, layout),
        out_shape=jax.ShapeDtypeStruct((CORES * layout.rows, LAGS), jnp.bfloat16),
        in_specs=[vmem] * 5,
        out_specs=vmem,
        scratch_shapes=[partner, pltpu.VMEM((CORES * layout.rows, LAGS), jnp.float32)],
        compiler_params=params,
        name="far",
    )(far, *kept)
    shape = (peers, 1, PAIRS, layout.stations, LAGS)
    return result.reshape(shape).transpose(0, 3, 1, 2, 4)


def solution(mesh):
    placed = (P("blk", None, None, "band"), P("blk", None))
    return jax.shard_map(
        body,
        mesh=mesh,
        in_specs=placed,
        out_specs=P(None, "blk", "band", None, None),
        check_vma=False,
    )
```

```python
import functools
import math

import jax
import jax.numpy as jnp
from jax import lax
from jax.experimental import pallas as pl
from jax.experimental.pallas import tpu as pltpu
from jax.sharding import PartitionSpec as P

F = 320
FIRST = 15
NFFT = 1500
MAXLAG = 64
LAGS = 2 * MAXLAG
LANES = 128
COMPONENTS = 3
PAIRS = COMPONENTS * COMPONENTS
ROWS = 8
CORES = 2
VMEM_LIMIT = 40 * 1024 * 1024


class Layout:
    def __init__(self, stations, bins, bands, peers):
        self.stations = stations
        self.bins = bins
        self.bands = bands
        self.peers = peers
        self.halves = peers // CORES
        self.slots = self.halves * bands
        self.whole = bins // LANES
        self.rest = bins % LANES
        self.rest_row = 2 * COMPONENTS * self.whole
        self.main = bands * 2 * self.whole
        self.per = LANES // (2 * self.rest)
        self.tails = -(-bands // self.per)
        self.depth = (self.main + self.tails) * LANES
        self.groups = stations * PAIRS
        self.rows = self.groups * self.halves
        assert stations == bands and stations % 2 == 0 and bins % ROWS == 0
        assert 0 < self.rest and COMPONENTS * self.rest <= LANES
        assert self.rest_row + 2 <= ROWS

    def row(self, component, chunk):
        return 2 * (component * self.whole + chunk)

    def slot(self, half, band):
        return (half * self.bands + band + 1) % self.slots

    def crossed(self, half):
        return half < self.halves // 2

    def bands_of(self, tail):
        return range(tail * self.per, min((tail + 1) * self.per, self.bands))


def pack_kernel(layout, quality_ref, spectra_ref, pieces_ref, wide):
    stations = layout.stations
    if layout.rest_row + 2 < ROWS:
        wide[...] = jnp.zeros_like(wide)
    for s in range(stations):
        rests = jnp.zeros((2, LANES), jnp.float32)
        for a in range(COMPONENTS):
            usable = quality_ref[s, a].astype(jnp.float32)
            both = spectra_ref[s, a].astype(jnp.float32) * usable
            for chunk in range(layout.whole):
                row = s * ROWS + 2 * (a * layout.whole + chunk)
                wide[row : row + 2, :] = both[:, chunk * LANES : (chunk + 1) * LANES]
            rest = both[:, layout.whole * LANES :]
            padded = jnp.concatenate([rest, jnp.zeros((2, LANES - layout.rest), jnp.float32)], axis=1)
            rests = rests + (pltpu.roll(padded, a * layout.rest, 1) if a else padded)
        row = s * ROWS + layout.rest_row
        wide[row : row + 2, :] = rests
    packed = [wide[s * ROWS : (s + 1) * ROWS, :] for s in range(stations)]
    for band in range(layout.bands):
        order = [packed[(band + k) % stations] for k in range(stations)]
        piece = jnp.concatenate(order).astype(jnp.bfloat16)
        for half in range(layout.halves):
            pieces_ref[layout.slot(half, band)] = piece


def at_block(layout, rows, component, block):
    shift = ((block - component) * layout.rest) % LANES
    return pltpu.roll(rows, shift, 1) if shift else rows


def lag_table(layout, anchors, table_ref):
    steps = 2 * lax.broadcasted_iota(jnp.int32, (ROWS, LAGS), 1) - 2 * MAXLAG + 1

    def wave(bins):
        index = lax.rem(bins * steps, 2 * NFFT)
        phases = math.pi / NFFT * index.astype(jnp.float32)
        return jnp.cos(phases), jnp.sin(phases)

    sublane = lax.broadcasted_iota(jnp.int32, (ROWS, LAGS), 0)
    near_cos, near_sin = wave(sublane)
    count = layout.bins * layout.bands // ROWS
    padded = -(-count // ROWS)
    for block in range(padded):
        cosine, sine = wave((sublane + block * ROWS) * ROWS + FIRST)
        anchors[0, block * ROWS : (block + 1) * ROWS, :] = cosine / math.sqrt(F)
        anchors[1, block * ROWS : (block + 1) * ROWS, :] = sine / math.sqrt(F)

    def put(chunk, values):
        high = values.astype(jnp.bfloat16)
        low = (values - high.astype(jnp.float32)).astype(jnp.bfloat16)
        many, place = (layout.main, chunk) if chunk < layout.main else (layout.tails, layout.main + chunk)
        for start in (place * LANES, (place + many) * LANES):
            table_ref[start : start + LANES, :LAGS] = high
            table_ref[start : start + LANES, LAGS:] = low

    def pair(first, bins):
        cosines, sines = [], []
        for g in range(first // ROWS, (first + bins) // ROWS):
            cosine = anchors[0, g : g + 1, :]
            sine = anchors[1, g : g + 1, :]
            cosines.append(cosine * near_cos - sine * near_sin)
            sines.append(-(sine * near_cos + cosine * near_sin))
        return jnp.concatenate(cosines), jnp.concatenate(sines)

    for band in range(layout.bands):
        for chunk in range(layout.whole):
            cosine, sine = pair(band * layout.bins + chunk * LANES, LANES)
            put(2 * (band * layout.whole + chunk), cosine)
            put(2 * (band * layout.whole + chunk) + 1, sine)
    for tail in range(layout.tails):
        parts = []
        for band in layout.bands_of(tail):
            parts.extend(pair(band * layout.bins + layout.whole * LANES, layout.rest))
        spare = LANES - len(parts) * layout.rest
        if spare:
            parts.append(jnp.zeros((spare, LAGS), jnp.float32))
        put(layout.main + tail, jnp.concatenate(parts))


def own_rows(layout, pieces_ref, own, rest_ref):
    stations = layout.stations
    here = lax.div(lax.axis_index("blk"), CORES) * layout.bands
    place = lax.axis_index("band")
    for band in range(layout.bands):
        piece = pieces_ref[lax.rem(here + band + 1, layout.slots)].astype(jnp.float32)
        for k in range(stations):
            start = pl.multiple_of((band * stations + lax.rem(place + k, stations)) * ROWS, ROWS)
            own[pl.ds(start, ROWS), :] = piece[k * ROWS : (k + 1) * ROWS]
    block = lax.div(lax.broadcasted_iota(jnp.int32, (1, LANES), 1), layout.rest)
    for tail in range(layout.tails):
        for i in range(stations):
            for a in range(COMPONENTS):
                with_real = with_imag = jnp.zeros((1, LANES), jnp.float32)
                for k, band in enumerate(layout.bands_of(tail)):
                    row = (band * stations + i) * ROWS + layout.rest_row
                    real = own[row : row + 1, :]
                    imag = own[row + 1 : row + 2, :]
                    first, second = block == 2 * k, block == 2 * k + 1
                    with_real = jnp.where(first, at_block(layout, real, a, 2 * k), with_real)
                    with_real = jnp.where(second, at_block(layout, imag, a, 2 * k + 1), with_real)
                    with_imag = jnp.where(first, at_block(layout, imag, a, 2 * k), with_imag)
                    with_imag = jnp.where(second, -at_block(layout, real, a, 2 * k + 1), with_imag)
                to = 2 * ((tail * stations + i) * COMPONENTS + a)
                rest_ref[to : to + 1, :] = with_real
                rest_ref[to + 1 : to + 2, :] = with_imag


def correlated(layout, pieces_ref, table_ref, own, rests, partner):
    for half in range(layout.halves):
        for band in range(layout.bands):
            row = (half * layout.bands + band) * ROWS
            partner[row : row + ROWS, :] = pieces_ref[layout.slot(half, band)].astype(jnp.float32)[:ROWS]

    def partner_rows(band, row):
        return partner[pl.ds(band * ROWS + row, layout.halves, stride=layout.bands * ROWS), :]

    values = []
    for band in range(layout.bands):
        for chunk in range(layout.whole):
            reals, imags = [], []
            for b in range(COMPONENTS):
                z_real = partner_rows(band, layout.row(b, chunk))
                z_imag = partner_rows(band, layout.row(b, chunk) + 1)
                for a in range(COMPONENTS):
                    for i in range(layout.stations):
                        row = (band * layout.stations + i) * ROWS + layout.row(a, chunk)
                        x_real = own[row : row + 1, :]
                        x_imag = own[row + 1 : row + 2, :]
                        reals.append(x_real * z_real + x_imag * z_imag)
                        imags.append(x_imag * z_real - x_real * z_imag)
            values.append(jnp.concatenate(reals))
            values.append(jnp.concatenate(imags))
    block = lax.div(lax.broadcasted_iota(jnp.int32, (1, LANES), 1), layout.rest)
    for tail in range(layout.tails):
        rows = [
            (partner_rows(band, layout.rest_row), partner_rows(band, layout.rest_row + 1))
            for band in layout.bands_of(tail)
        ]
        parts = []
        for b in range(COMPONENTS):
            z_real = z_imag = None
            for k, (real, imag) in enumerate(rows):
                for place in (2 * k, 2 * k + 1):
                    turned_real = at_block(layout, real, b, place)
                    turned_imag = at_block(layout, imag, b, place)
                    z_real = turned_real if z_real is None else jnp.where(block >= place, turned_real, z_real)
                    z_imag = turned_imag if z_imag is None else jnp.where(block >= place, turned_imag, z_imag)
            for a in range(COMPONENTS):
                for i in range(layout.stations):
                    row = 2 * ((tail * layout.stations + i) * COMPONENTS + a)
                    parts.append(rests[row : row + 1, :] * z_real + rests[row + 1 : row + 2, :] * z_imag)
        values.append(jnp.concatenate(parts))
    highs = [value.astype(jnp.bfloat16) for value in values]
    lows = [(value - high.astype(jnp.float32)).astype(jnp.bfloat16) for value, high in zip(values, highs)]
    main = layout.main
    left = jnp.concatenate(highs[:main] + lows[:main] + highs[main:] + lows[main:], axis=1)
    both = jnp.dot(left, table_ref[...], preferred_element_type=jnp.float32)
    return both[:, :LAGS] + both[:, LAGS:]


def near_kernel(layout, pieces_ref, sums_ref, table_ref, own_ref, rest_ref, partner, anchors):
    lag_table(layout, anchors, table_ref)
    own_rows(layout, pieces_ref, own_ref, rest_ref)
    sums_ref[...] = correlated(layout, pieces_ref, table_ref, own_ref, rest_ref, partner)


def far_kernel(layout, pieces_ref, near_ref, table_ref, own_ref, rest_ref, out_ref, partner, sums):
    far = correlated(layout, pieces_ref, table_ref, own_ref, rest_ref, partner)
    blk = lax.axis_index("blk")
    core = lax.rem(blk, CORES)
    team = jnp.where(layout.crossed(lax.div(blk, CORES)), 1 - core, core)
    halves = lax.broadcasted_iota(jnp.int32, (layout.halves, LAGS), 0)
    near_first = layout.crossed(halves).astype(jnp.int32) == team
    for b in range(COMPONENTS):
        for a in range(COMPONENTS):
            for i in range(layout.stations):
                group = (b * COMPONENTS + a) * layout.stations + i
                rows = slice(group * layout.halves, (group + 1) * layout.halves)
                for origin in range(CORES):
                    taken = near_first if origin == 0 else jnp.logical_not(near_first)
                    first = origin * layout.groups + (a * COMPONENTS + b) * layout.stations + i
                    to = pl.ds(first, layout.halves, stride=CORES * layout.groups)
                    sums[to, :] = jnp.where(taken, near_ref[rows, :], far[rows])
    out_ref[...] = sums[...].astype(jnp.bfloat16)


def body(spectra, quality):
    peers = lax.axis_size("blk")
    bands = lax.axis_size("band")
    layout = Layout(spectra.shape[0], spectra.shape[3], bands, peers)
    vmem = pl.BlockSpec(memory_space=pltpu.VMEM)
    params = pltpu.CompilerParams(vmem_limit_bytes=VMEM_LIMIT)
    piece_rows = layout.stations * ROWS
    pieces = pl.pallas_call(
        functools.partial(pack_kernel, layout),
        out_shape=pltpu.VMEM((layout.slots, piece_rows, LANES), jnp.bfloat16),
        in_specs=[pl.BlockSpec(memory_space=pltpu.SMEM), vmem],
        out_specs=vmem,
        scratch_shapes=[pltpu.VMEM((piece_rows, LANES), jnp.float32)],
        name="pack",
    )(quality, spectra)
    groups = [[0] * layout.slots for _ in range(CORES)]
    for half in range(layout.halves):
        for core in range(CORES):
            team = 1 - core if layout.crossed(half) else core
            for band in range(bands):
                groups[team][layout.slot(half, band)] = (half * CORES + core) * bands + band
    near = lax.all_to_all(
        pieces, ("blk", "band"), split_axis=0, concat_axis=0, tiled=True, axis_index_groups=groups
    )
    far = lax.ppermute(near[:, :ROWS], "blk", [(i, i ^ 1) for i in range(peers)])
    partner = pltpu.VMEM((layout.slots * ROWS, LANES), jnp.float32)
    kept = pl.pallas_call(
        functools.partial(near_kernel, layout),
        out_shape=(
            pltpu.VMEM((layout.rows, LAGS), jnp.float32),
            pltpu.VMEM((2 * layout.depth, 2 * LAGS), jnp.bfloat16),
            pltpu.VMEM((bands * layout.stations * ROWS, LANES), jnp.float32),
            pltpu.VMEM((2 * layout.tails * layout.stations * COMPONENTS, LANES), jnp.float32),
        ),
        in_specs=[vmem],
        out_specs=(vmem,) * 4,
        scratch_shapes=[
            partner,
            pltpu.VMEM((2, -(-layout.bins * bands // (ROWS * ROWS)) * ROWS, LAGS), jnp.float32),
        ],
        compiler_params=params,
        cost_estimate=pl.CostEstimate(flops=10**8, bytes_accessed=10**6, transcendentals=0),
        name="near",
    )(near)
    result = pl.pallas_call(
        functools.partial(far_kernel, layout),
        out_shape=jax.ShapeDtypeStruct((CORES * layout.rows, LAGS), jnp.bfloat16),
        in_specs=[vmem] * 5,
        out_specs=vmem,
        scratch_shapes=[partner, pltpu.VMEM((CORES * layout.rows, LAGS), jnp.float32)],
        compiler_params=params,
        name="far",
    )(far, *kept)
    shape = (peers, 1, PAIRS, layout.stations, LAGS)
    return result.reshape(shape).transpose(0, 3, 1, 2, 4)


def solution(mesh):
    placed = (P("blk", None, None, "band"), P("blk", None))
    return jax.shard_map(
        body,
        mesh=mesh,
        in_specs=placed,
        out_specs=P(None, "blk", "band", None, None),
        check_vma=False,
    )
```

```python
import functools
import math

import jax
import jax.numpy as jnp
from jax import lax
from jax.experimental import pallas as pl
from jax.experimental.pallas import tpu as pltpu
from jax.sharding import PartitionSpec as P

F = 320
FIRST = 15
NFFT = 1500
MAXLAG = 64
LAGS = 2 * MAXLAG
LANES = 128
COMPONENTS = 3
PAIRS = COMPONENTS * COMPONENTS
ROWS = 8
CORES = 2
VMEM_LIMIT = 40 * 1024 * 1024


class Layout:
    def __init__(self, stations, bins, bands, peers):
        self.stations = stations
        self.bins = bins
        self.bands = bands
        self.peers = peers
        self.halves = peers // CORES
        self.slots = self.halves * bands
        self.whole = bins // LANES
        self.rest = bins % LANES
        self.rest_row = 2 * COMPONENTS * self.whole
        self.main = bands * 2 * self.whole
        self.per = LANES // (2 * self.rest)
        self.tails = -(-bands // self.per)
        self.depth = (self.main + self.tails) * LANES
        self.groups = stations * PAIRS
        self.rows = self.groups * self.halves
        assert stations == bands and stations % 2 == 0 and bins % ROWS == 0
        assert 0 < self.rest and COMPONENTS * self.rest <= LANES
        assert self.rest_row + 2 <= ROWS

    def row(self, component, chunk):
        return 2 * (component * self.whole + chunk)

    def slot(self, half, band):
        return (half * self.bands + band + 1) % self.slots

    def crossed(self, half):
        return half < self.halves // 2

    def bands_of(self, tail):
        return range(tail * self.per, min((tail + 1) * self.per, self.bands))


def pack_kernel(layout, quality_ref, spectra_ref, pieces_ref, wide):
    stations = layout.stations
    spare = jnp.zeros((2, LANES - layout.rest), jnp.float32)
    raw = []
    for s in range(stations):
        for a in range(COMPONENTS):
            both = spectra_ref[s * COMPONENTS + a].astype(jnp.float32)
            rest = jnp.concatenate([both[:, layout.whole * LANES :], spare], axis=1)
            raw.append((both, pltpu.roll(rest, a * layout.rest, 1) if a else rest))
    if layout.rest_row + 2 < ROWS:
        wide[...] = jnp.zeros_like(wide)
    for s in range(stations):
        rests = None
        for a in range(COMPONENTS):
            usable = quality_ref[s, a].astype(jnp.float32)
            both, rest = raw[s * COMPONENTS + a]
            for chunk in range(layout.whole):
                row = s * ROWS + layout.row(a, chunk)
                wide[row : row + 2, :] = both[:, chunk * LANES : (chunk + 1) * LANES] * usable
            rests = rest * usable if rests is None else rests + rest * usable
        row = s * ROWS + layout.rest_row
        wide[row : row + 2, :] = rests
    packed = [wide[s * ROWS : (s + 1) * ROWS, :] for s in range(stations)]
    for band in range(layout.bands):
        order = [packed[(band + k) % stations] for k in range(stations)]
        piece = jnp.concatenate(order).astype(jnp.bfloat16)
        for half in range(layout.halves):
            pieces_ref[layout.slot(half, band)] = piece


def at_block(layout, rows, component, block):
    shift = ((block - component) * layout.rest) % LANES
    return pltpu.roll(rows, shift, 1) if shift else rows


def lag_table(layout, anchors, table_ref):
    steps = 2 * lax.broadcasted_iota(jnp.int32, (ROWS, LAGS), 1) - 2 * MAXLAG + 1

    def wave(bins):
        index = lax.rem(bins * steps, 2 * NFFT)
        phases = math.pi / NFFT * index.astype(jnp.float32)
        return jnp.cos(phases), jnp.sin(phases)

    sublane = lax.broadcasted_iota(jnp.int32, (ROWS, LAGS), 0)
    near_cos, near_sin = wave(sublane)
    count = layout.bins * layout.bands // ROWS
    padded = -(-count // ROWS)
    for block in range(padded):
        cosine, sine = wave((sublane + block * ROWS) * ROWS + FIRST)
        anchors[0, block * ROWS : (block + 1) * ROWS, :] = cosine / math.sqrt(F)
        anchors[1, block * ROWS : (block + 1) * ROWS, :] = sine / math.sqrt(F)

    def put(chunk, values):
        high = values.astype(jnp.bfloat16)
        low = (values - high.astype(jnp.float32)).astype(jnp.bfloat16)
        many, place = (layout.main, chunk) if chunk < layout.main else (layout.tails, layout.main + chunk)
        for start in (place * LANES, (place + many) * LANES):
            table_ref[start : start + LANES, :LAGS] = high
            table_ref[start : start + LANES, LAGS:] = low

    def pair(first, bins):
        cosines, sines = [], []
        for g in range(first // ROWS, (first + bins) // ROWS):
            cosine = anchors[0, g : g + 1, :]
            sine = anchors[1, g : g + 1, :]
            cosines.append(cosine * near_cos - sine * near_sin)
            sines.append(-(sine * near_cos + cosine * near_sin))
        return jnp.concatenate(cosines), jnp.concatenate(sines)

    for band in range(layout.bands):
        for chunk in range(layout.whole):
            cosine, sine = pair(band * layout.bins + chunk * LANES, LANES)
            put(2 * (band * layout.whole + chunk), cosine)
            put(2 * (band * layout.whole + chunk) + 1, sine)
    for tail in range(layout.tails):
        parts = []
        for band in layout.bands_of(tail):
            parts.extend(pair(band * layout.bins + layout.whole * LANES, layout.rest))
        spare = LANES - len(parts) * layout.rest
        if spare:
            parts.append(jnp.zeros((spare, LAGS), jnp.float32))
        put(layout.main + tail, jnp.concatenate(parts))


def own_rows(layout, pieces_ref, own, rest_ref):
    stations = layout.stations
    here = lax.div(lax.axis_index("blk"), CORES) * layout.bands
    place = lax.axis_index("band")
    for band in range(layout.bands):
        piece = pieces_ref[lax.rem(here + band + 1, layout.slots)].astype(jnp.float32)
        for k in range(stations):
            start = pl.multiple_of((band * stations + lax.rem(place + k, stations)) * ROWS, ROWS)
            own[pl.ds(start, ROWS), :] = piece[k * ROWS : (k + 1) * ROWS]
    block = lax.div(lax.broadcasted_iota(jnp.int32, (1, LANES), 1), layout.rest)
    for tail in range(layout.tails):
        for i in range(stations):
            for a in range(COMPONENTS):
                with_real = with_imag = jnp.zeros((1, LANES), jnp.float32)
                for k, band in enumerate(layout.bands_of(tail)):
                    row = (band * stations + i) * ROWS + layout.rest_row
                    real = own[row : row + 1, :]
                    imag = own[row + 1 : row + 2, :]
                    first, second = block == 2 * k, block == 2 * k + 1
                    with_real = jnp.where(first, at_block(layout, real, a, 2 * k), with_real)
                    with_real = jnp.where(second, at_block(layout, imag, a, 2 * k + 1), with_real)
                    with_imag = jnp.where(first, at_block(layout, imag, a, 2 * k), with_imag)
                    with_imag = jnp.where(second, -at_block(layout, real, a, 2 * k + 1), with_imag)
                to = 2 * ((tail * stations + i) * COMPONENTS + a)
                rest_ref[to : to + 1, :] = with_real
                rest_ref[to + 1 : to + 2, :] = with_imag


def correlated(layout, pieces_ref, table_ref, own, rests, partner):
    for half in range(layout.halves):
        for band in range(layout.bands):
            row = (half * layout.bands + band) * ROWS
            partner[row : row + ROWS, :] = pieces_ref[layout.slot(half, band)].astype(jnp.float32)[:ROWS]

    def partner_rows(band, row):
        return partner[pl.ds(band * ROWS + row, layout.halves, stride=layout.bands * ROWS), :]

    values = []
    for band in range(layout.bands):
        for chunk in range(layout.whole):
            reals, imags = [], []
            for b in range(COMPONENTS):
                z_real = partner_rows(band, layout.row(b, chunk))
                z_imag = partner_rows(band, layout.row(b, chunk) + 1)
                for a in range(COMPONENTS):
                    for i in range(layout.stations):
                        row = (band * layout.stations + i) * ROWS + layout.row(a, chunk)
                        x_real = own[row : row + 1, :]
                        x_imag = own[row + 1 : row + 2, :]
                        reals.append(x_real * z_real + x_imag * z_imag)
                        imags.append(x_imag * z_real - x_real * z_imag)
            values.append(jnp.concatenate(reals))
            values.append(jnp.concatenate(imags))
    block = lax.div(lax.broadcasted_iota(jnp.int32, (1, LANES), 1), layout.rest)
    for tail in range(layout.tails):
        rows = [
            (partner_rows(band, layout.rest_row), partner_rows(band, layout.rest_row + 1))
            for band in layout.bands_of(tail)
        ]
        parts = []
        for b in range(COMPONENTS):
            z_real = z_imag = None
            for k, (real, imag) in enumerate(rows):
                for place in (2 * k, 2 * k + 1):
                    turned_real = at_block(layout, real, b, place)
                    turned_imag = at_block(layout, imag, b, place)
                    z_real = turned_real if z_real is None else jnp.where(block >= place, turned_real, z_real)
                    z_imag = turned_imag if z_imag is None else jnp.where(block >= place, turned_imag, z_imag)
            for a in range(COMPONENTS):
                for i in range(layout.stations):
                    row = 2 * ((tail * layout.stations + i) * COMPONENTS + a)
                    parts.append(rests[row : row + 1, :] * z_real + rests[row + 1 : row + 2, :] * z_imag)
        values.append(jnp.concatenate(parts))
    highs = [value.astype(jnp.bfloat16) for value in values]
    lows = [(value - high.astype(jnp.float32)).astype(jnp.bfloat16) for value, high in zip(values, highs)]
    main = layout.main
    left = jnp.concatenate(highs[:main] + lows[:main] + highs[main:] + lows[main:], axis=1)
    both = jnp.dot(left, table_ref[...], preferred_element_type=jnp.float32)
    return both[:, :LAGS] + both[:, LAGS:]


def near_kernel(layout, pieces_ref, sums_ref, table_ref, own_ref, rest_ref, partner, anchors):
    lag_table(layout, anchors, table_ref)
    own_rows(layout, pieces_ref, own_ref, rest_ref)
    sums_ref[...] = correlated(layout, pieces_ref, table_ref, own_ref, rest_ref, partner)


def far_kernel(layout, pieces_ref, near_ref, table_ref, own_ref, rest_ref, out_ref, partner, sums):
    far = correlated(layout, pieces_ref, table_ref, own_ref, rest_ref, partner)
    blk = lax.axis_index("blk")
    core = lax.rem(blk, CORES)
    team = jnp.where(layout.crossed(lax.div(blk, CORES)), 1 - core, core)
    halves = lax.broadcasted_iota(jnp.int32, (layout.halves, LAGS), 0)
    near_first = layout.crossed(halves).astype(jnp.int32) == team
    for b in range(COMPONENTS):
        for a in range(COMPONENTS):
            for i in range(layout.stations):
                group = (b * COMPONENTS + a) * layout.stations + i
                rows = slice(group * layout.halves, (group + 1) * layout.halves)
                for origin in range(CORES):
                    taken = near_first if origin == 0 else jnp.logical_not(near_first)
                    first = origin * layout.groups + (a * COMPONENTS + b) * layout.stations + i
                    to = pl.ds(first, layout.halves, stride=CORES * layout.groups)
                    sums[to, :] = jnp.where(taken, near_ref[rows, :], far[rows])
    out_ref[...] = sums[...].astype(jnp.bfloat16)


def body(spectra, quality):
    peers = lax.axis_size("blk")
    bands = lax.axis_size("band")
    layout = Layout(spectra.shape[0], spectra.shape[3], bands, peers)
    vmem = pl.BlockSpec(memory_space=pltpu.VMEM)
    params = pltpu.CompilerParams(vmem_limit_bytes=VMEM_LIMIT)
    piece_rows = layout.stations * ROWS
    pieces = pl.pallas_call(
        functools.partial(pack_kernel, layout),
        out_shape=pltpu.VMEM((layout.slots, piece_rows, LANES), jnp.bfloat16),
        in_specs=[pl.BlockSpec(memory_space=pltpu.SMEM), vmem],
        out_specs=vmem,
        scratch_shapes=[pltpu.VMEM((piece_rows, LANES), jnp.float32)],
        name="pack",
    )(quality, spectra.reshape(-1, 2, spectra.shape[3]))
    groups = [[0] * layout.slots for _ in range(CORES)]
    for half in range(layout.halves):
        for core in range(CORES):
            team = 1 - core if layout.crossed(half) else core
            for band in range(bands):
                groups[team][layout.slot(half, band)] = (half * CORES + core) * bands + band
    near = lax.all_to_all(
        pieces, ("blk", "band"), split_axis=0, concat_axis=0, tiled=True, axis_index_groups=groups
    )
    far = lax.ppermute(near[:, :ROWS], "blk", [(i, i ^ 1) for i in range(peers)])
    partner = pltpu.VMEM((layout.slots * ROWS, LANES), jnp.float32)
    kept = pl.pallas_call(
        functools.partial(near_kernel, layout),
        out_shape=(
            pltpu.VMEM((layout.rows, LAGS), jnp.float32),
            pltpu.VMEM((2 * layout.depth, 2 * LAGS), jnp.bfloat16),
            pltpu.VMEM((bands * layout.stations * ROWS, LANES), jnp.float32),
            pltpu.VMEM((2 * layout.tails * layout.stations * COMPONENTS, LANES), jnp.float32),
        ),
        in_specs=[vmem],
        out_specs=(vmem,) * 4,
        scratch_shapes=[
            partner,
            pltpu.VMEM((2, -(-layout.bins * bands // (ROWS * ROWS)) * ROWS, LAGS), jnp.float32),
        ],
        compiler_params=params,
        cost_estimate=pl.CostEstimate(flops=10**8, bytes_accessed=10**6, transcendentals=0),
        name="near",
    )(near)
    result = pl.pallas_call(
        functools.partial(far_kernel, layout),
        out_shape=jax.ShapeDtypeStruct((CORES * layout.rows, LAGS), jnp.bfloat16),
        in_specs=[vmem] * 5,
        out_specs=vmem,
        scratch_shapes=[partner, pltpu.VMEM((CORES * layout.rows, LAGS), jnp.float32)],
        compiler_params=params,
        name="far",
    )(far, *kept)
    shape = (peers, 1, PAIRS, layout.stations, LAGS)
    return result.reshape(shape).transpose(0, 3, 1, 2, 4)


def solution(mesh):
    placed = (P("blk", None, None, "band"), P("blk", None))
    return jax.shard_map(
        body,
        mesh=mesh,
        in_specs=placed,
        out_specs=P(None, "blk", "band", None, None),
        check_vma=False,
    )
```
